32 devices in a mesh: blk: 16 (over z, x, core), win: 2 (over y).
Axes of the slice: x: 2, y: 2, z: 4, core: 2. Of those that a mesh axis runs over, the one named last changes fastest.
Arguments:
- traces: bfloat16 [8, 512, 8192], P('win', None, 'blk'), may hold values from -256 to 256, as said below
- channel_mask: int32 [8192], P('blk'), may hold values 0 or 1
Outputs:
- cross: float32 [4, 2, 2, 8192, 512], P(None, 'win', None, 'blk')
The draws below stay inside these ranges and needn't reach their ends.
Inputs may be any that keep to these rules, and one draw needn't show every extreme that they name: traces are noise records of the channels with different amplitudes.
All inputs are finite; a program needn't handle non-finite values. No bound on the sum of `channel_mask` on one device may be relied on, other than what follows from the above.
Results may differ from the reference program's by a relative error of at most 0.0049.
Values may be sent and summed in bfloat16 or wider, within the bound.
A program may use at most 64 MiB of HBM per device.

```python
import math
import jax
import jax.numpy as jnp
from jax import lax

SAMPLES = 512
CH_BLK = 512
ROUNDS = 4
BAND = 128
WINDOWS = 8
CHANNELS = 8192
N_BLK = 16
N_WIN = 2


def draw_traces(key, part):
    key = jax.random.fold_in(key, 11)
    key_noise, key_chan, key_win = jax.random.split(key, 3)
    noise = jnp.clip(jax.random.normal(key_noise, (WINDOWS, SAMPLES + 1, CHANNELS), jnp.float32), -4.0, 4.0)
    top_scale = 10.0
    chan_scale = jnp.exp(jax.random.uniform(key_chan, (CHANNELS,), jnp.float32, 0.0, jnp.log(top_scale)))
    win_scale = jnp.exp(jax.random.uniform(key_win, (WINDOWS, CHANNELS), jnp.float32, jnp.log(0.5), jnp.log(2.0)))
    colored = noise[:, 1:] - 0.6 * noise[:, :-1]
    values = colored * chan_scale[None, None, :] * win_scale[:, None, :]
    return values.astype(jnp.bfloat16)


def with_ends(array, own_key, least, top_value):
    extent = array.shape
    index_at = [jax.random.randint(jax.random.fold_in(own_key, axis), (), 0, extent[axis]) for axis in range(len(extent))]
    array = array.at[tuple(index_at)].set(least)
    longest = extent.index(max(extent))
    index_at[longest] = (index_at[longest] + 1) % extent[longest]
    return array.at[tuple(index_at)].set(top_value)


def setup_inputs(seed: int = 0) -> dict:
    key_of = jax.random.split(jax.random.key(seed), 3)
    return {
        "traces": draw_traces(jax.random.fold_in(key_of[2], 71), 0),
        "channel_mask": with_ends((jax.random.randint(key_of[1], (CHANNELS,), 0, 8) < 7).astype(jnp.int32), jax.random.fold_in(key_of[1], 1), 0, 1),
    }


water_level = 0.5

def dft_table(samples_len, band_count):
    row_index = jnp.arange(samples_len, dtype=jnp.int32)
    per_band = samples_len // band_count
    half_rows = per_band // 2
    freq_bin = row_index // per_band * half_rows + row_index % per_band % half_rows
    imag_rows = row_index % per_band >= half_rows
    time_index = jnp.arange(samples_len, dtype=jnp.int32)
    phase_int = freq_bin[:, None] * time_index[None, :] % samples_len
    angles = 2.0 * math.pi / samples_len * phase_int.astype(jnp.float32)
    hann_taper = 0.5 - 0.5 * jnp.cos(2.0 * math.pi / samples_len * time_index.astype(jnp.float32))
    entries = jnp.where(imag_rows[:, None], -jnp.sin(angles), jnp.cos(angles)) * hann_taper[None, :]
    return entries.astype(jnp.bfloat16)

def reference(traces, channel_mask):
    transform = dft_table(SAMPLES, N_WIN)
    spectra = jnp.einsum('rt,wtc->wrc', transform.astype(jnp.float32), traces.astype(jnp.float32)).astype(jnp.bfloat16)
    spec_f32 = spectra.astype(jnp.float32).reshape(WINDOWS, N_WIN, 2, BAND, CHANNELS)
    power_mean = lax.optimization_barrier(jnp.mean(spec_f32[:, :, 0] ** 2 + spec_f32[:, :, 1] ** 2, axis=0))
    level_mean = lax.optimization_barrier(jnp.mean(power_mean, axis=(0, 1)))
    factor = channel_mask.astype(jnp.float32)[None, None, :] / jnp.sqrt(power_mean + water_level * level_mean[None, None, :] + 1e-06)
    white = (spec_f32 * factor[None, :, None]).astype(jnp.bfloat16).reshape(WINDOWS, SAMPLES, CHANNELS)
    norm_scale = 1.0 / math.sqrt(WINDOWS * BAND)
    rounds_out = []
    for offset in range(1, ROUNDS + 1):
        partner = jnp.roll(white, -offset * CH_BLK, axis=2)
        bands_out = []
        for band_id in range(N_WIN):
            lower = band_id * 2 * BAND
            upper = lower + 2 * BAND
            own_rows = white[:, lower:upper].astype(jnp.float32).reshape(WINDOWS, 2 * BAND, N_BLK, CH_BLK)
            far_rows = partner[:, lower:upper].astype(jnp.float32).reshape(WINDOWS, 2 * BAND, N_BLK, CH_BLK)
            swapped = jnp.concatenate([far_rows[:, BAND:], -far_rows[:, :BAND]], axis=1)
            real_part = jnp.einsum('wqnc,wqnd->ncd', own_rows, far_rows).reshape(CHANNELS, CH_BLK)
            imag_part = jnp.einsum('wqnc,wqnd->ncd', own_rows, swapped).reshape(CHANNELS, CH_BLK)
            bands_out.append(jnp.stack([real_part, imag_part]) * norm_scale)
        rounds_out.append(jnp.stack(bands_out))
    return jnp.stack(rounds_out)
```

```python
import functools
import math

import jax
import jax.numpy as jnp
import ml_dtypes
import numpy as np
from jax import lax
from jax.experimental import pallas as pl
from jax.experimental.pallas import tpu as pltpu
from jax.sharding import PartitionSpec as P

ROUNDS = 4
CHUNK_BINS = 16
WATER_LEVEL = 0.5
MESH = pl.DeviceIdType.MESH


def dft_table(samples, bands, bins):
    width = samples // 2 // bands
    order = np.arange(samples // 2).reshape(bands, width // bins, 1, bins)
    order = np.broadcast_to(order, (bands, width // bins, 2, bins))
    time = np.arange(samples)
    phase = order[..., None] * time % samples
    angles = 2.0 * np.pi / samples * phase
    taper = 0.5 - 0.5 * np.cos(2.0 * np.pi / samples * time)
    imag = np.array([False, True])[None, None, :, None, None]
    entries = np.where(imag, -np.sin(angles), np.cos(angles)) * taper
    return entries.reshape(bands, 2 * width, samples).astype(np.float32).astype(ml_dtypes.bfloat16)


def kernel(
    blocks, bands, traces, table, mask, acc,
    buf, stage, gathered, level,
    send_y, recv_y, send_z, send_x, send_sib, recv_blk,
    send_lw, recv_lw, send_lb, recv_lb,
):
    me = lax.axis_index("blk")
    band = lax.axis_index("win")
    core = lax.rem(me, 2)
    odd = lax.rem(me // 2, 2)
    local_windows = traces.shape[0]
    chunks, windows, rows, channels = buf.shape[1:]
    bins = rows // 2
    bin_count = chunks * bins * bands

    def at(step):
        return (lax.rem(me + step + blocks, blocks), band)

    def peer(step):
        return (me, lax.rem(band + step, bands))

    sibling = (me + 1 - 2 * core, band)
    others = [at(s) for s in range(-ROUNDS, ROUNDS + 1) if s] + [peer(d) for d in range(1, bands)]
    barrier = pltpu.get_barrier_semaphore()
    for other in others:
        pl.semaphore_signal(barrier, inc=1, device_id=other, device_id_type=MESH)

    def remote(src, dst, send, recv, target):
        return pltpu.make_async_remote_copy(
            src_ref=src, dst_ref=dst, send_sem=send, recv_sem=recv,
            device_id=target, device_id_type=MESH,
        )

    def copy_y(d, q):
        first = (bands - d) * local_windows
        return remote(
            stage.at[d - 1, q], buf.at[0, q, pl.ds(first, local_windows)],
            send_y.at[d - 1, q], recv_y.at[d - 1, q], peer(d),
        )

    def copy_z(q):
        return remote(buf.at[0, q], buf.at[4, q], send_z.at[q], recv_blk.at[3, q], at(-4))

    def copy_x(slot, step, q):
        return remote(buf.at[slot, q], buf.at[2, q], send_x.at[q], recv_blk.at[1, q], at(step))

    def copy_sib(slot, pair, q):
        return remote(
            buf.at[slot, q], buf.at[1 + 2 * pair, q],
            send_sib.at[pair, q], recv_blk.at[2 * pair, q], sibling,
        )

    def spectrum(which, window):
        rows_of = jnp.dot(table[which], traces[window], preferred_element_type=jnp.float32)
        return rows_of.astype(jnp.bfloat16).reshape(chunks, rows, channels)

    def power(spec):
        total = None
        for w in range(windows):
            re, im = spec(w)
            term = re * re + im * im
            total = term if total is None else total + term
        return total * (1.0 / windows)

    def parts(slot, q):
        def get(w):
            value = buf[slot, q, w].astype(jnp.float32)
            return value[:bins], value[bins:]
        return get

    def own(q):
        for d in range(1, bands):
            copy_y(d, q).wait_recv()
        copy_z(q).start()

        @pl.when(odd == 1)
        def _():
            copy_x(0, -2, q).start()

        @pl.when(core == 1)
        def _():
            copy_sib(0, 0, q).start()

        gathered[0] += power(parts(0, q)).reshape(bins // 8, 8, channels).sum(axis=0)

    def relay(q):
        copy_z(q).wait_recv()

        @pl.when(odd == 0)
        def _():
            copy_x(4, 2, q).start()

        @pl.when(core == 0)
        def _():
            copy_sib(4, 1, q).start()

    def forward(q):
        copy_x(0, -2, q).wait_recv()
        copy_sib(2, core, q).start()

    def factor(slot, spec):
        mean = jnp.sum(level[slot, 0], axis=0, keepdims=True) * (1.0 / bin_count)
        return level[slot, 1][:1] * lax.rsqrt(power(spec) + WATER_LEVEL * mean + 1e-06)

    def cross(q, first):
        spec = parts(0, q)
        scale = factor(0, spec)
        lhs = []
        for w in range(windows):
            re, im = spec(w)
            re, im = re * scale, im * scale
            lhs.append(jnp.concatenate([
                jnp.concatenate([re, -im], axis=1), jnp.concatenate([im, re], axis=1)
            ], axis=0).astype(jnp.bfloat16))
        lhs = jnp.concatenate(lhs, axis=0).T
        for slot in (2, 4, 1, 3):
            if slot in (1, 3):
                copy_sib(0, slot // 2, q).wait_recv()
            spec = parts(slot, q)
            scale = factor(slot, spec)
            rhs = []
            for w in range(windows):
                re, im = spec(w)
                rhs.append(jnp.concatenate([re * scale, im * scale], axis=0).astype(jnp.bfloat16))
            acc[slot - 1] += jnp.dot(
                lhs, jnp.concatenate(rhs, axis=0), preferred_element_type=jnp.float32
            )

    for d in range(1, bands):
        which = lax.rem(band + d, bands)
        for w in range(local_windows):
            stage[d - 1, :, w] = spectrum(which, w)
    pl.semaphore_wait(barrier, len(others))
    for q in range(chunks):
        for d in range(1, bands):
            copy_y(d, q).start()
    for w in range(local_windows):
        buf[0, :, w] = spectrum(band, w)
    gathered[0] = jnp.zeros(gathered.shape[1:], jnp.float32)

    early = (chunks - 1) // 2
    for q in range(chunks):
        own(q)
        if q >= 2 and q % 2 == 0:
            relay(q // 2 - 1)
            if q >= 4:
                forward(q // 2 - 2)

    def copy_lw(d):
        return remote(
            gathered.at[0], gathered.at[bands - d], send_lw.at[d - 1], recv_lw.at[d - 1], peer(d)
        )

    def copy_lb(r):
        return remote(level.at[0], level.at[r], send_lb.at[r - 1], recv_lb.at[r - 1], at(-r))

    for d in range(1, bands):
        copy_lw(d).start()
    level[0, 1] = jnp.broadcast_to(mask[...].astype(jnp.float32), (8, channels))
    for slot in range(ROUNDS):
        acc[slot] = jnp.zeros(acc.shape[1:], jnp.float32)
    for d in range(1, bands):
        copy_lw(d).wait()
    level[0, 0] = jnp.sum(gathered[...], axis=0)
    for r in range(1, ROUNDS + 1):
        copy_lb(r).start()
    for r in range(1, ROUNDS + 1):
        copy_lb(r).wait()

    def late(t, _):
        @pl.when(t < chunks)
        def _():
            relay(t)

        @pl.when((t >= 1) & (t <= chunks))
        def _():
            forward(t - 1)

        @pl.when(t >= 2)
        def _():
            cross(t - 2, False)
        return 0

    if early > 2:
        def catch_up(q, _):
            cross(q, False)
            return 0
        lax.fori_loop(0, early - 2, catch_up, 0)
    lax.fori_loop(early, chunks + 2, late, 0)

    for q in range(chunks):
        for d in range(1, bands):
            copy_y(d, q).wait_send()
        copy_z(q).wait_send()
        copy_x(0, -2, q).wait_send()
        copy_sib(0, 0, q).wait_send()
        copy_sib(0, 1, q).wait_send()


def local(blocks, bands, traces, channel_mask):
    local_windows, samples, channels = traces.shape
    windows = local_windows * bands
    width = samples // 2 // bands
    bins = min(CHUNK_BINS, width)
    chunks = width // bins
    table = jnp.asarray(dft_table(samples, bands, bins))
    vmem = pl.BlockSpec(memory_space=pltpu.VMEM)
    dma = pltpu.SemaphoreType.DMA
    flops = 2 * samples * samples * channels * local_windows
    flops += 2 * ROUNDS * 2 * channels * channels * windows * 2 * width
    acc = pl.pallas_call(
        functools.partial(kernel, blocks, bands),
        out_shape=jax.ShapeDtypeStruct((ROUNDS, 2 * channels, channels), jnp.float32),
        in_specs=[vmem] * 3,
        out_specs=vmem,
        scratch_shapes=[
            pltpu.VMEM((ROUNDS + 1, chunks, windows, 2 * bins, channels), jnp.bfloat16),
            pltpu.VMEM((bands - 1, chunks, local_windows, 2 * bins, channels), jnp.bfloat16),
            pltpu.VMEM((bands, 8, channels), jnp.float32),
            pltpu.VMEM((ROUNDS + 1, 2, 8, channels), jnp.float32),
            dma((bands - 1, chunks)), dma((bands - 1, chunks)),
            dma((chunks,)), dma((chunks,)), dma((2, chunks)), dma((ROUNDS, chunks)),
            dma((bands - 1,)), dma((bands - 1,)), dma((ROUNDS,)), dma((ROUNDS,)),
        ],
        compiler_params=pltpu.CompilerParams(
            collective_id=0, has_side_effects=True, vmem_limit_bytes=48 * 2**20
        ),
        cost_estimate=pl.CostEstimate(flops=flops, bytes_accessed=2**24, transcendentals=0),
    )(traces, table, channel_mask[None])
    norm_scale = 1.0 / math.sqrt(windows * width)
    return (acc * norm_scale).reshape(ROUNDS, 1, 2, channels, channels)


def solution(mesh):
    return jax.shard_map(
        functools.partial(local, mesh.shape["blk"], mesh.shape["win"]),
        mesh=mesh,
        in_specs=(P("win", None, "blk"), P("blk")),
        out_specs=P(None, "win", None, "blk", None),
        check_vma=False,
    )
```

```python
import functools
import math

import jax
import jax.numpy as jnp
import ml_dtypes
import numpy as np
from jax import lax
from jax.experimental import pallas as pl
from jax.experimental.pallas import tpu as pltpu
from jax.sharding import PartitionSpec as P

ROUNDS = 4
CHUNK_BINS = 16
WATER_LEVEL = 0.5
MESH = pl.DeviceIdType.MESH


def dft_table(samples, bands, bins):
    width = samples // 2 // bands
    order = np.arange(samples // 2).reshape(bands, width // bins, 1, bins)
    order = np.broadcast_to(order, (bands, width // bins, 2, bins))
    time = np.arange(samples)
    phase = order[..., None] * time % samples
    angles = 2.0 * np.pi / samples * phase
    taper = 0.5 - 0.5 * np.cos(2.0 * np.pi / samples * time)
    imag = np.array([False, True])[None, None, :, None, None]
    entries = np.where(imag, -np.sin(angles), np.cos(angles)) * taper
    return entries.reshape(bands, 2 * width, samples).astype(np.float32).astype(ml_dtypes.bfloat16)


DEPTH = 3


def kernel(
    blocks, bands, traces, table, mask, out,
    buf, stage, acc, gathered, level,
    send_y, recv_y, send_z, send_x, send_sib, recv_blk,
    send_lw, recv_lw, send_lb, recv_lb, send_out,
):
    me = lax.axis_index("blk")
    band = lax.axis_index("win")
    core = lax.rem(me, 2)
    odd = lax.rem(me // 2, 2)
    pieces, local_windows, rows, channels = buf.shape[1:]
    chunks = pieces // bands
    windows = local_windows * bands
    bins = rows // 2
    bin_count = chunks * bins * bands
    relay_lag = DEPTH
    forward_lag = relay_lag + 2
    cross_lag = -(-forward_lag // bands)

    def at(step):
        return (lax.rem(me + step + blocks, blocks), band)

    def peer(step):
        return (me, lax.rem(band + step, bands))

    sibling = (me + 1 - 2 * core, band)
    others = [at(s) for s in range(-ROUNDS, ROUNDS + 1) if s] + [peer(d) for d in range(1, bands)]
    barrier = pltpu.get_barrier_semaphore()
    for other in others:
        pl.semaphore_signal(barrier, inc=1, device_id=other, device_id_type=MESH)

    def remote(src, dst, send, recv, target):
        return pltpu.make_async_remote_copy(
            src_ref=src, dst_ref=dst, send_sem=send, recv_sem=recv,
            device_id=target, device_id_type=MESH,
        )

    def copy_y(d, q):
        return remote(
            stage.at[d - 1, q], buf.at[0, q * bands + bands - d],
            send_y.at[d - 1, q], recv_y.at[d - 1, q], peer(d),
        )

    def copy_z(u):
        return remote(buf.at[0, u], buf.at[4, u], send_z.at[u], recv_blk.at[3, u], at(-4))

    def copy_x(slot, step, u):
        return remote(buf.at[slot, u], buf.at[2, u], send_x.at[u], recv_blk.at[1, u], at(step))

    def copy_sib(slot, pair, u):
        return remote(
            buf.at[slot, u], buf.at[1 + 2 * pair, u],
            send_sib.at[pair, u], recv_blk.at[2 * pair, u], sibling,
        )

    def copy_lw(d):
        return remote(
            gathered.at[0], gathered.at[bands - d], send_lw.at[d - 1], recv_lw.at[d - 1], peer(d)
        )

    def copy_lb(r):
        return remote(level.at[0], level.at[r], send_lb.at[r - 1], recv_lb.at[r - 1], at(-r))

    def copy_out(r):
        return pltpu.make_async_copy(acc.at[r], out.at[r], send_out.at[r])

    def spectrum(which, window):
        value = jnp.dot(table[which], traces[window], preferred_element_type=jnp.float32)
        value = value.astype(jnp.bfloat16)
        wide = value.astype(jnp.float32)
        gathered[0] += (wide * wide).reshape(-1, 8, channels).sum(axis=0)
        return value.reshape(chunks, rows, channels)

    def parts(slot, q):
        def get(w):
            piece = q * bands + w // local_windows
            value = buf[slot, piece, w % local_windows].astype(jnp.float32)
            return value[:bins], value[bins:]
        return get

    def factor(slot, spec):
        total = None
        for w in range(windows):
            re, im = spec(w)
            term = re * re + im * im
            total = term if total is None else total + term
        power = total * (1.0 / windows)
        mean = jnp.sum(level[slot, 0], axis=0, keepdims=True) * (1.0 / (windows * bin_count))
        return level[slot, 1][:1] * lax.rsqrt(power + WATER_LEVEL * mean + 1e-06)

    def cross(q):
        spec = parts(0, q)
        scale = factor(0, spec)
        lhs = []
        for w in range(windows):
            re, im = spec(w)
            re, im = re * scale, im * scale
            lhs.append(jnp.concatenate([
                jnp.concatenate([re, -im], axis=1), jnp.concatenate([im, re], axis=1)
            ], axis=0).astype(jnp.bfloat16))
        lhs = jnp.concatenate(lhs, axis=0).T
        for slot in (2, 4, 1, 3):
            if slot in (1, 3):
                for h in range(bands):
                    copy_sib(0, slot // 2, q * bands + h).wait_recv()
            spec = parts(slot, q)
            scale = factor(slot, spec)
            rhs = []
            for w in range(windows):
                re, im = spec(w)
                rhs.append(jnp.concatenate([re * scale, im * scale], axis=0).astype(jnp.bfloat16))
            acc[slot - 1] += jnp.dot(
                lhs, jnp.concatenate(rhs, axis=0), preferred_element_type=jnp.float32
            )

            @pl.when(q == chunks - 1)
            def _():
                copy_out(slot - 1).start()

    gathered[0] = jnp.zeros(gathered.shape[1:], jnp.float32)
    for d in range(1, bands):
        which = lax.rem(band + d, bands)
        for w in range(local_windows):
            stage[d - 1, :, w] = spectrum(which, w)
    pl.semaphore_wait(barrier, len(others))
    for q in range(min(2, chunks)):
        for d in range(bands - 1, 0, -1):
            copy_y(d, q).start()
    for w in range(local_windows):
        value = spectrum(band, w)
        for q in range(chunks):
            buf[0, q * bands, w] = value[q]
    level[0, 1] = jnp.broadcast_to(mask[...].astype(jnp.float32), (8, channels))

    def send_own(t, h):
        u = t * bands + h
        if h:
            copy_y(bands - h, t).wait_recv()

        @pl.when(u >= DEPTH)
        def _():
            copy_z(u - DEPTH).wait_send()

        copy_z(u).start()

        @pl.when(odd == 1)
        def _():
            copy_x(0, -2, u).start()

        @pl.when(core == 1)
        def _():
            copy_sib(0, 0, u).start()

    def relay(u):
        copy_z(u).wait_recv()

        @pl.when(odd == 0)
        def _():
            copy_x(4, 2, u).start()

        @pl.when(core == 0)
        def _():
            copy_sib(4, 1, u).start()

    def forward(u):
        copy_x(0, -2, u).wait_recv()
        copy_sib(2, core, u).start()

    def step(t, _):
        for h in range(bands):
            u = t * bands + h

            @pl.when(t < chunks)
            def _():
                send_own(t, h)

            if h == bands - 1:
                @pl.when(t + 2 < chunks)
                def _():
                    for d in range(bands - 1, 0, -1):
                        copy_y(d, t + 2).start()

            @pl.when((u >= relay_lag) & (u < pieces + relay_lag))
            def _():
                relay(u - relay_lag)

            @pl.when((u >= forward_lag) & (u < pieces + forward_lag))
            def _():
                forward(u - forward_lag)

        @pl.when(t == 0)
        def _():
            for d in range(1, bands):
                copy_lw(d).start()
            for slot in range(ROUNDS):
                acc[slot] = jnp.zeros(acc.shape[1:], jnp.float32)
            for d in range(1, bands):
                copy_lw(d).wait()
            level[0, 0] = jnp.sum(gathered[...], axis=0)
            for r in range(1, ROUNDS + 1):
                copy_lb(r).start()

        @pl.when(t == cross_lag)
        def _():
            for r in range(1, ROUNDS + 1):
                copy_lb(r).wait()

        @pl.when(t >= cross_lag)
        def _():
            cross(t - cross_lag)
        return 0

    lax.fori_loop(0, chunks + cross_lag, step, 0)

    for q in range(chunks):
        for d in range(1, bands):
            copy_y(d, q).wait_send()
    for u in range(pieces):
        if u >= pieces - DEPTH:
            copy_z(u).wait_send()
        copy_x(0, -2, u).wait_send()
        copy_sib(0, 0, u).wait_send()
        copy_sib(0, 1, u).wait_send()
    for r in range(ROUNDS):
        copy_out(r).wait()


def local(blocks, bands, traces, channel_mask):
    local_windows, samples, channels = traces.shape
    windows = local_windows * bands
    width = samples // 2 // bands
    bins = min(CHUNK_BINS, width)
    chunks = width // bins
    pieces = chunks * bands
    table = jnp.asarray(dft_table(samples, bands, bins))
    vmem = pl.BlockSpec(memory_space=pltpu.VMEM)
    dma = pltpu.SemaphoreType.DMA
    flops = 2 * samples * samples * channels * local_windows
    flops += 2 * ROUNDS * 2 * channels * channels * windows * 2 * width
    acc = pl.pallas_call(
        functools.partial(kernel, blocks, bands),
        out_shape=jax.ShapeDtypeStruct((ROUNDS, 2 * channels, channels), jnp.float32),
        in_specs=[vmem] * 3,
        out_specs=pl.BlockSpec(memory_space=pl.ANY),
        scratch_shapes=[
            pltpu.VMEM((ROUNDS + 1, pieces, local_windows, 2 * bins, channels), jnp.bfloat16),
            pltpu.VMEM((bands - 1, chunks, local_windows, 2 * bins, channels), jnp.bfloat16),
            pltpu.VMEM((ROUNDS, 2 * channels, channels), jnp.float32),
            pltpu.VMEM((bands, 8, channels), jnp.float32),
            pltpu.VMEM((ROUNDS + 1, 2, 8, channels), jnp.float32),
            dma((bands - 1, chunks)), dma((bands - 1, chunks)),
            dma((pieces,)), dma((pieces,)), dma((2, pieces)), dma((ROUNDS, pieces)),
            dma((bands - 1,)), dma((bands - 1,)), dma((ROUNDS,)), dma((ROUNDS,)), dma((ROUNDS,)),
        ],
        compiler_params=pltpu.CompilerParams(
            collective_id=0, has_side_effects=True, vmem_limit_bytes=32 * 2**20
        ),
        cost_estimate=pl.CostEstimate(flops=flops, bytes_accessed=2**24, transcendentals=0),
    )(traces, table, channel_mask[None])
    norm_scale = 1.0 / math.sqrt(windows * width)
    return (acc * norm_scale).reshape(ROUNDS, 1, 2, channels, channels)


def solution(mesh):
    return jax.shard_map(
        functools.partial(local, mesh.shape["blk"], mesh.shape["win"]),
        mesh=mesh,
        in_specs=(P("win", None, "blk"), P("blk")),
        out_specs=P(None, "win", None, "blk", None),
        check_vma=False,
    )
```

```python
import functools
import math

import jax
import jax.numpy as jnp
import ml_dtypes
import numpy as np
from jax import lax
from jax.experimental import pallas as pl
from jax.experimental.pallas import tpu as pltpu
from jax.sharding import PartitionSpec as P

ROUNDS = 4
CHUNK_BINS = 8
WATER_LEVEL = 0.5
MESH = pl.DeviceIdType.MESH


def dft_table(samples, bands, bins):
    width = samples // 2 // bands
    order = np.arange(samples // 2).reshape(bands, width // bins, 1, bins)
    order = np.broadcast_to(order, (bands, width // bins, 2, bins))
    time = np.arange(samples)
    phase = order[..., None] * time % samples
    angles = 2.0 * np.pi / samples * phase
    taper = 0.5 - 0.5 * np.cos(2.0 * np.pi / samples * time)
    imag = np.array([False, True])[None, None, :, None, None]
    entries = np.where(imag, -np.sin(angles), np.cos(angles)) * taper
    return entries.reshape(bands, 2 * width, samples).astype(np.float32).astype(ml_dtypes.bfloat16)


DEPTH = 4


def kernel(
    blocks, bands, traces, table, mask, acc,
    buf, stage, gathered, level,
    send_y, recv_y, send_z, send_x, send_sib, recv_blk,
    send_lw, recv_lw, send_lb, recv_lb,
):
    me = lax.axis_index("blk")
    band = lax.axis_index("win")
    core = lax.rem(me, 2)
    odd = lax.rem(me // 2, 2)
    pieces, local_windows, rows, channels = buf.shape[1:]
    chunks = pieces // bands
    windows = local_windows * bands
    bins = rows // 2
    bin_count = chunks * bins * bands
    relay_lag = DEPTH
    forward_lag = relay_lag + 2
    cross_lag = -(-forward_lag // bands)

    def at(step):
        return (lax.rem(me + step + blocks, blocks), band)

    def peer(step):
        return (me, lax.rem(band + step, bands))

    sibling = (me + 1 - 2 * core, band)
    others = [at(s) for s in range(-ROUNDS, ROUNDS + 1) if s] + [peer(d) for d in range(1, bands)]
    barrier = pltpu.get_barrier_semaphore()
    for other in others:
        pl.semaphore_signal(barrier, inc=1, device_id=other, device_id_type=MESH)

    def remote(src, dst, send, recv, target):
        return pltpu.make_async_remote_copy(
            src_ref=src, dst_ref=dst, send_sem=send, recv_sem=recv,
            device_id=target, device_id_type=MESH,
        )

    def copy_y(d, q):
        return remote(
            stage.at[d - 1, q], buf.at[0, q * bands + bands - d],
            send_y.at[d - 1, q], recv_y.at[d - 1, q], peer(d),
        )

    def copy_z(u):
        return remote(buf.at[0, u], buf.at[4, u], send_z.at[u], recv_blk.at[3, u], at(-4))

    def copy_x(slot, step, u):
        return remote(buf.at[slot, u], buf.at[2, u], send_x.at[u], recv_blk.at[1, u], at(step))

    def copy_sib(slot, pair, u):
        return remote(
            buf.at[slot, u], buf.at[1 + 2 * pair, u],
            send_sib.at[pair, u], recv_blk.at[2 * pair, u], sibling,
        )

    def copy_lw(d):
        return remote(
            gathered.at[0], gathered.at[bands - d], send_lw.at[d - 1], recv_lw.at[d - 1], peer(d)
        )

    def copy_lb(r):
        return remote(level.at[0], level.at[r], send_lb.at[r - 1], recv_lb.at[r - 1], at(-r))

    def spectrum(which, window):
        value = jnp.dot(table[which], traces[window], preferred_element_type=jnp.float32)
        value = value.astype(jnp.bfloat16)
        wide = value.astype(jnp.float32)
        gathered[0] += (wide * wide).reshape(-1, 8, channels).sum(axis=0)
        return value.reshape(chunks, rows, channels)

    def parts(slot, q):
        def get(w):
            piece = q * bands + w // local_windows
            value = buf[slot, piece, w % local_windows].astype(jnp.float32)
            return value[:bins], value[bins:]
        return get

    def factor(slot, spec):
        total = None
        for w in range(windows):
            re, im = spec(w)
            term = re * re + im * im
            total = term if total is None else total + term
        power = total * (1.0 / windows)
        mean = jnp.sum(level[slot, 0], axis=0, keepdims=True) * (1.0 / (windows * bin_count))
        return level[slot, 1][:1] * lax.rsqrt(power + WATER_LEVEL * mean + 1e-06)

    def cross(q):
        spec = parts(0, q)
        scale = factor(0, spec)
        lhs = []
        for w in range(windows):
            re, im = spec(w)
            re, im = re * scale, im * scale
            lhs.append(jnp.concatenate([
                jnp.concatenate([re, -im], axis=1), jnp.concatenate([im, re], axis=1)
            ], axis=0).astype(jnp.bfloat16))
        lhs = jnp.concatenate(lhs, axis=0).T
        for slot in (2, 4, 1, 3):
            if slot in (1, 3):
                for h in range(bands):
                    copy_sib(0, slot // 2, q * bands + h).wait_recv()
            spec = parts(slot, q)
            scale = factor(slot, spec)
            rhs = []
            for w in range(windows):
                re, im = spec(w)
                rhs.append(jnp.concatenate([re * scale, im * scale], axis=0).astype(jnp.bfloat16))
            acc[slot - 1] += jnp.dot(
                lhs, jnp.concatenate(rhs, axis=0), preferred_element_type=jnp.float32
            )

    gathered[0] = jnp.zeros(gathered.shape[1:], jnp.float32)
    for d in range(1, bands):
        which = lax.rem(band + d, bands)
        for w in range(local_windows):
            stage[d - 1, :, w] = spectrum(which, w)
    pl.semaphore_wait(barrier, len(others))
    for q in range(min(2, chunks)):
        for d in range(bands - 1, 0, -1):
            copy_y(d, q).start()
    for w in range(local_windows):
        value = spectrum(band, w)
        for q in range(chunks):
            buf[0, q * bands, w] = value[q]
    level[0, 1] = jnp.broadcast_to(mask[...].astype(jnp.float32), (8, channels))

    def send_own(t, h):
        u = t * bands + h
        if h:
            copy_y(bands - h, t).wait_recv()

        @pl.when(u >= DEPTH)
        def _():
            copy_z(u - DEPTH).wait_send()

        copy_z(u).start()

        @pl.when(odd == 1)
        def _():
            copy_x(0, -2, u).start()

        @pl.when(core == 1)
        def _():
            copy_sib(0, 0, u).start()

    def relay(u):
        copy_z(u).wait_recv()

        @pl.when(odd == 0)
        def _():
            copy_x(4, 2, u).start()

        @pl.when(core == 0)
        def _():
            copy_sib(4, 1, u).start()

    def forward(u):
        copy_x(0, -2, u).wait_recv()
        copy_sib(2, core, u).start()

    def step(t, _):
        for h in range(bands):
            u = t * bands + h

            @pl.when(t < chunks)
            def _():
                send_own(t, h)

            if h == bands - 1:
                @pl.when(t + 2 < chunks)
                def _():
                    for d in range(bands - 1, 0, -1):
                        copy_y(d, t + 2).start()

            @pl.when((u >= relay_lag) & (u < pieces + relay_lag))
            def _():
                relay(u - relay_lag)

            @pl.when((u >= forward_lag) & (u < pieces + forward_lag))
            def _():
                forward(u - forward_lag)

        @pl.when(t == 0)
        def _():
            for d in range(1, bands):
                copy_lw(d).start()
            for slot in range(ROUNDS):
                acc[slot] = jnp.zeros(acc.shape[1:], jnp.float32)
            for d in range(1, bands):
                copy_lw(d).wait()
            level[0, 0] = jnp.sum(gathered[...], axis=0)
            for r in range(1, ROUNDS + 1):
                copy_lb(r).start()

        @pl.when(t == cross_lag)
        def _():
            for r in range(1, ROUNDS + 1):
                copy_lb(r).wait()

        @pl.when(t >= cross_lag)
        def _():
            cross(t - cross_lag)
        return 0

    lax.fori_loop(0, chunks + cross_lag, step, 0)

    for q in range(chunks):
        for d in range(1, bands):
            copy_y(d, q).wait_send()
    for u in range(pieces):
        if u >= pieces - DEPTH:
            copy_z(u).wait_send()
        copy_x(0, -2, u).wait_send()
        copy_sib(0, 0, u).wait_send()
        copy_sib(0, 1, u).wait_send()


def local(blocks, bands, traces, channel_mask):
    local_windows, samples, channels = traces.shape
    windows = local_windows * bands
    width = samples // 2 // bands
    bins = min(CHUNK_BINS, width)
    chunks = width // bins
    pieces = chunks * bands
    table = jnp.asarray(dft_table(samples, bands, bins))
    vmem = pl.BlockSpec(memory_space=pltpu.VMEM)
    dma = pltpu.SemaphoreType.DMA
    flops = 2 * samples * samples * channels * local_windows
    flops += 2 * ROUNDS * 2 * channels * channels * windows * 2 * width
    acc = pl.pallas_call(
        functools.partial(kernel, blocks, bands),
        out_shape=jax.ShapeDtypeStruct((ROUNDS, 2 * channels, channels), jnp.float32),
        in_specs=[vmem] * 3,
        out_specs=vmem,
        scratch_shapes=[
            pltpu.VMEM((ROUNDS + 1, pieces, local_windows, 2 * bins, channels), jnp.bfloat16),
            pltpu.VMEM((bands - 1, chunks, local_windows, 2 * bins, channels), jnp.bfloat16),
            pltpu.VMEM((bands, 8, channels), jnp.float32),
            pltpu.VMEM((ROUNDS + 1, 2, 8, channels), jnp.float32),
            dma((bands - 1, chunks)), dma((bands - 1, chunks)),
            dma((pieces,)), dma((pieces,)), dma((2, pieces)), dma((ROUNDS, pieces)),
            dma((bands - 1,)), dma((bands - 1,)), dma((ROUNDS,)), dma((ROUNDS,)),
        ],
        compiler_params=pltpu.CompilerParams(
            collective_id=0, has_side_effects=True, vmem_limit_bytes=32 * 2**20
        ),
        cost_estimate=pl.CostEstimate(flops=flops, bytes_accessed=2**24, transcendentals=0),
    )(traces, table, channel_mask[None])
    norm_scale = 1.0 / math.sqrt(windows * width)
    return (acc * norm_scale).reshape(ROUNDS, 1, 2, channels, channels)


def solution(mesh):
    return jax.shard_map(
        functools.partial(local, mesh.shape["blk"], mesh.shape["win"]),
        mesh=mesh,
        in_specs=(P("win", None, "blk"), P("blk")),
        out_specs=P(None, "win", None, "blk", None),
        check_vma=False,
    )
```

```python
import functools
import math

import jax
import jax.numpy as jnp
import ml_dtypes
import numpy as np
from jax import lax
from jax.experimental import pallas as pl
from jax.experimental.pallas import tpu as pltpu
from jax.sharding import PartitionSpec as P

ROUNDS = 4
CHUNK_BINS = 8
WATER_LEVEL = 0.5
MESH = pl.DeviceIdType.MESH


def dft_table(samples, bands, bins):
    width = samples // 2 // bands
    order = np.arange(samples // 2).reshape(bands, width // bins, 1, bins)
    order = np.broadcast_to(order, (bands, width // bins, 2, bins))
    time = np.arange(samples)
    phase = order[..., None] * time % samples
    angles = 2.0 * np.pi / samples * phase
    taper = 0.5 - 0.5 * np.cos(2.0 * np.pi / samples * time)
    imag = np.array([False, True])[None, None, :, None, None]
    entries = np.where(imag, -np.sin(angles), np.cos(angles)) * taper
    return entries.reshape(bands, 2 * width, samples).astype(np.float32).astype(ml_dtypes.bfloat16)


DEPTH = 4


def kernel(
    blocks, bands, traces, table, mask, acc,
    buf, stage, gathered, level,
    send_y, recv_y, send_z, send_x, send_sib, recv_blk,
    send_lw, recv_lw, send_lb, recv_lb,
):
    me = lax.axis_index("blk")
    band = lax.axis_index("win")
    core = lax.rem(me, 2)
    odd = lax.rem(me // 2, 2)
    pieces, local_windows, rows, channels = buf.shape[1:]
    chunks = pieces // bands
    windows = local_windows * bands
    bins = rows // 2
    bin_count = chunks * bins * bands
    relay_lag = DEPTH
    forward_lag = relay_lag + 2
    cross_lag = -(-forward_lag // bands)

    def at(step):
        return (lax.rem(me + step + blocks, blocks), band)

    def peer(step):
        return (me, lax.rem(band + step, bands))

    sibling = (me + 1 - 2 * core, band)
    others = [at(s) for s in range(-ROUNDS, ROUNDS + 1) if s] + [peer(d) for d in range(1, bands)]
    barrier = pltpu.get_barrier_semaphore()
    for other in others:
        pl.semaphore_signal(barrier, inc=1, device_id=other, device_id_type=MESH)

    def remote(src, dst, send, recv, target):
        return pltpu.make_async_remote_copy(
            src_ref=src, dst_ref=dst, send_sem=send, recv_sem=recv,
            device_id=target, device_id_type=MESH,
        )

    def copy_y(d, q):
        return remote(
            stage.at[d - 1, q], buf.at[0, q * bands + bands - d],
            send_y.at[d - 1, q], recv_y.at[d - 1, q], peer(d),
        )

    def copy_z(u):
        return remote(buf.at[0, u], buf.at[4, u], send_z.at[u], recv_blk.at[3, u], at(-4))

    def copy_x(slot, step, u):
        return remote(buf.at[slot, u], buf.at[2, u], send_x.at[u], recv_blk.at[1, u], at(step))

    def copy_sib(slot, pair, u):
        return remote(
            buf.at[slot, u], buf.at[1 + 2 * pair, u],
            send_sib.at[pair, u], recv_blk.at[2 * pair, u], sibling,
        )

    def copy_lw(d):
        return remote(
            gathered.at[0], gathered.at[bands - d], send_lw.at[d - 1], recv_lw.at[d - 1], peer(d)
        )

    def copy_lb(r):
        return remote(level.at[0], level.at[r], send_lb.at[r - 1], recv_lb.at[r - 1], at(-r))

    def spectrum(which, window):
        value = jnp.dot(table[which], traces[window], preferred_element_type=jnp.float32)
        value = value.astype(jnp.bfloat16)
        wide = value.astype(jnp.float32)
        gathered[0] += (wide * wide).reshape(-1, 8, channels).sum(axis=0)
        return value.reshape(chunks, rows, channels)

    def parts(slot, q):
        def get(w):
            piece = q * bands + w // local_windows
            value = buf[slot, piece, w % local_windows].astype(jnp.float32)
            return value[:bins], value[bins:]
        return get

    def factor(slot, spec):
        total = None
        for w in range(windows):
            re, im = spec(w)
            term = re * re + im * im
            total = term if total is None else total + term
        power = total * (1.0 / windows)
        mean = jnp.sum(level[slot, 0], axis=0, keepdims=True) * (1.0 / (windows * bin_count))
        return level[slot, 1][:1] * lax.rsqrt(power + WATER_LEVEL * mean + 1e-06)

    def cross(q):
        spec = parts(0, q)
        scale = factor(0, spec)
        lhs = []
        for w in range(windows):
            re, im = spec(w)
            re, im = re * scale, im * scale
            lhs.append(jnp.concatenate([
                jnp.concatenate([re, -im], axis=1), jnp.concatenate([im, re], axis=1)
            ], axis=0).astype(jnp.bfloat16))
        lhs = jnp.concatenate(lhs, axis=0).T
        for slot in (2, 4, 1, 3):
            if slot in (1, 3):
                for h in range(bands):
                    copy_sib(0, slot // 2, q * bands + h).wait_recv()
            spec = parts(slot, q)
            scale = factor(slot, spec)
            rhs = []
            for w in range(windows):
                re, im = spec(w)
                rhs.append(jnp.concatenate([re * scale, im * scale], axis=0).astype(jnp.bfloat16))
            acc[slot - 1] += jnp.dot(
                lhs, jnp.concatenate(rhs, axis=0), preferred_element_type=jnp.float32
            )

    gathered[0] = jnp.zeros(gathered.shape[1:], jnp.float32)
    for d in range(1, bands):
        which = lax.rem(band + d, bands)
        for w in range(local_windows):
            stage[d - 1, :, w] = spectrum(which, w)
    pl.semaphore_wait(barrier, len(others))
    for q in range(min(2, chunks)):
        for d in range(bands - 1, 0, -1):
            copy_y(d, q).start()
    for w in range(local_windows):
        value = spectrum(band, w)
        for q in range(chunks):
            buf[0, q * bands, w] = value[q]
    level[0, 1] = jnp.broadcast_to(mask[...].astype(jnp.float32), (8, channels))

    def send_own(t, h):
        u = t * bands + h
        if h:
            copy_y(bands - h, t).wait_recv()

        @pl.when(u >= DEPTH)
        def _():
            copy_z(u - DEPTH).wait_send()

        copy_z(u).start()

        @pl.when(odd == 1)
        def _():
            copy_x(0, -2, u).start()

        @pl.when(core == 1)
        def _():
            copy_sib(0, 0, u).start()

    def relay(u):
        copy_z(u).wait_recv()

        @pl.when(odd == 0)
        def _():
            copy_x(4, 2, u).start()

        @pl.when(core == 0)
        def _():
            copy_sib(4, 1, u).start()

    def forward(u):
        copy_x(0, -2, u).wait_recv()
        copy_sib(2, core, u).start()

    def step(t, _):
        for h in range(bands):
            u = t * bands + h

            @pl.when(t < chunks)
            def _():
                send_own(t, h)

            if h == bands - 1:
                @pl.when(t + 2 < chunks)
                def _():
                    for d in range(bands - 1, 0, -1):
                        copy_y(d, t + 2).start()

            @pl.when((u >= relay_lag) & (u < pieces + relay_lag))
            def _():
                relay(u - relay_lag)

            @pl.when((u >= forward_lag) & (u < pieces + forward_lag))
            def _():
                forward(u - forward_lag)

        @pl.when(t == 0)
        def _():
            for d in range(1, bands):
                copy_lw(d).start()
            for slot in range(ROUNDS):
                acc[slot] = jnp.zeros(acc.shape[1:], jnp.float32)

        @pl.when(t == 1)
        def _():
            for d in range(1, bands):
                copy_lw(d).wait()
            level[0, 0] = jnp.sum(gathered[...], axis=0)
            for r in range(1, ROUNDS + 1):
                copy_lb(r).start()

        @pl.when(t == cross_lag)
        def _():
            for r in range(1, ROUNDS + 1):
                copy_lb(r).wait()

        @pl.when(t >= cross_lag)
        def _():
            cross(t - cross_lag)
        return 0

    lax.fori_loop(0, chunks + cross_lag, step, 0)

    for q in range(chunks):
        for d in range(1, bands):
            copy_y(d, q).wait_send()
    for u in range(pieces):
        if u >= pieces - DEPTH:
            copy_z(u).wait_send()
        copy_x(0, -2, u).wait_send()
        copy_sib(0, 0, u).wait_send()
        copy_sib(0, 1, u).wait_send()


def local(blocks, bands, traces, channel_mask):
    local_windows, samples, channels = traces.shape
    windows = local_windows * bands
    width = samples // 2 // bands
    bins = min(CHUNK_BINS, width)
    chunks = width // bins
    pieces = chunks * bands
    table = jnp.asarray(dft_table(samples, bands, bins))
    vmem = pl.BlockSpec(memory_space=pltpu.VMEM)
    dma = pltpu.SemaphoreType.DMA
    flops = 2 * samples * samples * channels * local_windows
    flops += 2 * ROUNDS * 2 * channels * channels * windows * 2 * width
    acc = pl.pallas_call(
        functools.partial(kernel, blocks, bands),
        out_shape=jax.ShapeDtypeStruct((ROUNDS, 2 * channels, channels), jnp.float32),
        in_specs=[vmem] * 3,
        out_specs=vmem,
        scratch_shapes=[
            pltpu.VMEM((ROUNDS + 1, pieces, local_windows, 2 * bins, channels), jnp.bfloat16),
            pltpu.VMEM((bands - 1, chunks, local_windows, 2 * bins, channels), jnp.bfloat16),
            pltpu.VMEM((bands, 8, channels), jnp.float32),
            pltpu.VMEM((ROUNDS + 1, 2, 8, channels), jnp.float32),
            dma((bands - 1, chunks)), dma((bands - 1, chunks)),
            dma((pieces,)), dma((pieces,)), dma((2, pieces)), dma((ROUNDS, pieces)),
            dma((bands - 1,)), dma((bands - 1,)), dma((ROUNDS,)), dma((ROUNDS,)),
        ],
        compiler_params=pltpu.CompilerParams(
            collective_id=0, has_side_effects=True, vmem_limit_bytes=32 * 2**20
        ),
        cost_estimate=pl.CostEstimate(flops=flops, bytes_accessed=2**24, transcendentals=0),
    )(traces, table, channel_mask[None])
    norm_scale = 1.0 / math.sqrt(windows * width)
    return (acc * norm_scale).reshape(ROUNDS, 1, 2, channels, channels)


def solution(mesh):
    return jax.shard_map(
        functools.partial(local, mesh.shape["blk"], mesh.shape["win"]),
        mesh=mesh,
        in_specs=(P("win", None, "blk"), P("blk")),
        out_specs=P(None, "win", None, "blk", None),
        check_vma=False,
    )
```
